32 devices in a mesh: cfg: 1, pair: 16 (over z, y, x), blk: 2 (over core).
Axes of the slice: x: 2, y: 2, z: 4, core: 2. Of those that a mesh axis runs over, the one named last changes fastest.
Arguments:
- elementals: bfloat16 [16, 8, 2, 65536], P('cfg', None, None, ('pair', 'blk')), may hold values from -0.079589844 to 0.079589844
- perambulator: bfloat16 [16, 2, 1024, 1024], P(('cfg', 'pair'), None, None, 'blk'), may hold values from -0.1875 to 0.1875
- pairs: int32 [16, 2], replicated, may hold values from 0 to 15, as said below
- elem_index: int32 [16, 24], replicated, may hold values from 0 to 7
- coef_code: int32 [16, 24, 4, 4], replicated, may hold values from -2 to 2
- term_count: int32 [16], replicated, may hold values from 12 to 24, as said below
Outputs:
- correlator: float32 [16, 2], P(('cfg', 'pair'))
The draws below stay inside these ranges and needn't reach their ends.
Inputs may be any that keep to these rules, and one draw needn't show every extreme that they name: `pairs`: pair p + 8 lists the two timeslices of pair p in reverse order; the two timeslices of a pair differ. `term_count`: some pair uses all 24 terms.
All inputs are finite; a program needn't handle non-finite values.
Results may differ from the reference program's by a relative error of at most 0.0057.
Values may be sent and summed in bfloat16 or wider, within the bound.
A program may use at most 64 MiB of HBM per device.

```python
import jax
import jax.numpy as jnp
from jax import lax

NV = 256
NS = 4
NOP = 8
NTERM = 24
ORD = 1024
NT = 16
PAIRS = 16


def draw_pairs(key, part):
    key_first, key_step = jax.random.split(jax.random.fold_in(key, 11))
    first = jax.random.randint(key_first, (PAIRS // 2,), 0, NT)
    step = jax.random.randint(key_step, (PAIRS // 2,), 1, NT)
    leading = jnp.arange(PAIRS // 2) == 0
    first = jnp.where(leading, NT - 1, first)
    step = jnp.where(leading, 1, step)
    second = (first + step) % NT
    lower = jnp.stack([first, second], 1)
    upper = jnp.stack([second, first], 1)
    return jnp.concatenate([lower, upper], 0).astype(jnp.int32)


def draw_term_count(key, part):
    key_count, key_where = jax.random.split(jax.random.fold_in(key, 23))
    counts = jax.random.randint(key_count, (PAIRS,), NTERM // 2, NTERM + 1)
    where = jax.random.randint(key_where, (), 0, PAIRS)
    counts = jnp.where(jnp.arange(PAIRS) == where, NTERM, counts)
    return counts.astype(jnp.int32)


def set_ends(result, rng, least, largest):
    extent = result.shape
    place = [jax.random.randint(jax.random.fold_in(rng, axis), (), 0, extent[axis]) for axis in range(len(extent))]
    result = result.at[tuple(place)].set(least)
    longest = extent.index(max(extent))
    place[longest] = (place[longest] + 1) % extent[longest]
    return result.at[tuple(place)].set(largest)


def levels(rng, shape, pieces, low, largest):
    factor_of = 1.0
    for position, parts in pieces:
        heights = jax.random.uniform(jax.random.fold_in(jax.random.fold_in(rng, 6), position), (parts,), jnp.float32, low / len(pieces), largest / len(pieces))
        factor_of = factor_of * jnp.repeat(jnp.exp(heights), shape[position] // parts).reshape((-1,) + (1,) * (len(shape) - 1 - position))
    return factor_of


def noise(rng, shape, scale, most, cuts=(), kind=jnp.bfloat16):
    loudness = levels(rng, shape, cuts, -0.22, 0.18) if cuts else 1.0
    array = jax.random.normal(rng, shape, jnp.float32) * scale * loudness
    return jnp.minimum(jnp.maximum(array, -most), most).astype(kind)


def setup_inputs(seed: int = 0, part: int = 0) -> dict:
    splits = jax.random.split(jax.random.key(seed), 7)
    own_keys = jax.random.split(jax.random.fold_in(splits[6], part), 7)
    return {
        "elementals": noise(own_keys[0], (NT, NOP, 2, NV * NV), 0.01, 0.079589844, ((3, 32),)),
        "perambulator": noise(own_keys[1], (PAIRS, 2, ORD, ORD), ORD ** -0.5, 0.1875, ((0, 16), (3, 2))),
        "pairs": draw_pairs(jax.random.fold_in(splits[6], 71), part),
        "elem_index": set_ends(jax.random.randint(splits[3], (PAIRS, NTERM), 0, NOP), jax.random.fold_in(splits[3], 1), 0, NOP - 1).astype(jnp.int32),
        "coef_code": set_ends(jax.random.randint(splits[4], (PAIRS, NTERM, NS, NS), -2, 3), jax.random.fold_in(splits[4], 1), -2, 2).astype(jnp.int32),
        "term_count": draw_term_count(jax.random.fold_in(splits[6], 71), part),
    }


def dress(elementals, propagator, first, index, codes, count):
    picked = elementals[first][index].reshape(NTERM, 2, NV, NV)
    used = (jnp.arange(NTERM) < count).astype(jnp.float32)
    weights = codes.astype(jnp.float32) * 0.5 * used[:, None, None]
    blocks = jnp.einsum("kab,kcij->caibj", weights, picked.astype(jnp.float32), precision=lax.Precision.HIGHEST)
    blocks = blocks.astype(jnp.bfloat16).reshape(2, ORD, ORD)
    real_part = jnp.dot(blocks[0], propagator[0], preferred_element_type=jnp.float32) - jnp.dot(blocks[1], propagator[1], preferred_element_type=jnp.float32)
    imag_part = jnp.dot(blocks[0], propagator[1], preferred_element_type=jnp.float32) + jnp.dot(blocks[1], propagator[0], preferred_element_type=jnp.float32)
    return jnp.stack([real_part, imag_part]).astype(jnp.bfloat16)


def reference(elementals, perambulator, pairs, elem_index, coef_code, term_count):
    half = PAIRS // 2

    def one_pair(lower):
        upper = lower + half
        dressed_low = dress(elementals, perambulator[lower], pairs[lower, 0], elem_index[lower], coef_code[lower], term_count[lower])
        dressed_up = dress(elementals, perambulator[upper], pairs[upper, 0], elem_index[upper], coef_code[upper], term_count[upper])
        products = jnp.einsum("zrc,ycr->zy", dressed_low.astype(jnp.float32), dressed_up.astype(jnp.float32), precision=lax.Precision.HIGHEST)
        return jnp.stack([products[0, 0] - products[1, 1], products[0, 1] + products[1, 0]])

    values = lax.map(one_pair, jnp.arange(half, dtype=jnp.int32))
    return jnp.concatenate([values, values], 0)
```

```python
import functools

import jax
import jax.numpy as jnp
from jax import lax
from jax.experimental import pallas as pl
from jax.experimental.pallas import tpu as pltpu
from jax.sharding import PartitionSpec as P

NV = 256
NS = 4
SUB = 16
MESH = pl.DeviceIdType.MESH


def dot(x, y):
    return jnp.dot(x, y, preferred_element_type=jnp.float32)


def kernel(
    peers,
    picked_ref,
    fold_ref,
    prop_ref,
    out_ref,
    ebuf,
    obuf,
    pbuf,
    dbuf,
    rbuf,
    tot,
    psem,
    lsem,
    esend,
    erecv,
    fsend,
    frecv,
    dsend,
    drecv,
    ssend,
    srecv,
):
    me = lax.axis_index("pair")
    core = lax.axis_index("blk")
    other = 1 - core
    hp = peers // 2
    half = me // hp
    place = me % hp
    mirror = (me + hp) % peers
    chunk = picked_ref.shape[1]
    depth = fold_ref.shape[1]
    groups = peers * 2 * chunk // depth
    hg = groups // 2
    hrows = NV // 2

    prop_copy = pltpu.make_async_copy(prop_ref, pbuf, psem)
    prop_copy.start()

    def slot(s, c):
        return ebuf.at[pl.ds(pl.multiple_of((s * 2 + c) * chunk, SUB), chunk)]

    own_copy = pltpu.make_async_copy(picked_ref.at[me], slot(me, core), lsem)
    own_copy.start()

    barrier = pltpu.get_barrier_semaphore()

    def greet(k, _):
        pl.semaphore_signal(
            barrier,
            inc=1,
            device_id={"pair": (me + k) % peers, "blk": core},
            device_id_type=MESH,
        )
        return 0

    lax.fori_loop(1, peers, greet, 0)
    for target in (me, mirror):
        pl.semaphore_signal(
            barrier, inc=1, device_id={"pair": target, "blk": other}, device_id_type=MESH
        )
    pl.semaphore_wait(barrier, peers + 1)

    def send_copy(target):
        return pltpu.make_async_remote_copy(
            src_ref=picked_ref.at[target],
            dst_ref=slot(me, core),
            send_sem=esend.at[target],
            recv_sem=erecv.at[me],
            device_id={"pair": target, "blk": core},
            device_id_type=MESH,
        )

    def arrived(source):
        return pltpu.make_async_remote_copy(
            src_ref=slot(source, core),
            dst_ref=slot(source, core),
            send_sem=esend.at[source],
            recv_sem=erecv.at[source],
            device_id={"pair": me, "blk": other},
            device_id_type=MESH,
        )

    def forward(source, src=None):
        return pltpu.make_async_remote_copy(
            src_ref=slot(source, core) if src is None else src,
            dst_ref=slot(source, core),
            send_sem=fsend.at[source],
            recv_sem=frecv.at[source],
            device_id={"pair": me, "blk": other},
            device_id_type=MESH,
        )

    def handed(source):
        return pltpu.make_async_remote_copy(
            src_ref=slot(source, other),
            dst_ref=slot(source, other),
            send_sem=fsend.at[source],
            recv_sem=frecv.at[source],
            device_id={"pair": me, "blk": other},
            device_id_type=MESH,
        )

    forward(me, picked_ref.at[me]).start()
    send_copy((1 - half) * hp + place).start()

    def send(k, _):
        step = (place + k) % hp
        send_copy((1 - half) * hp + step).start()
        send_copy(half * hp + step).start()
        return 0

    lax.fori_loop(1, hp, send, 0)
    own_copy.wait()

    def block_copy(h, a):
        x = (a + half) % 2
        place_there = 2 * core + x
        return pltpu.make_async_remote_copy(
            src_ref=dbuf.at[:, a, x, pl.ds(pl.multiple_of(h * hrows, hrows), hrows)],
            dst_ref=rbuf.at[:, place_there, pl.ds(pl.multiple_of(h * hrows, hrows), hrows)],
            send_sem=dsend.at[h * NS + a],
            recv_sem=drecv.at[h * NS + place_there],
            device_id={"pair": mirror, "blk": a // 2},
            device_id_type=MESH,
        )

    def block_arrived(h, a):
        rows = pl.ds(pl.multiple_of(h * hrows, hrows), hrows)
        return pltpu.make_async_remote_copy(
            src_ref=rbuf.at[:, a, rows],
            dst_ref=rbuf.at[:, a, rows],
            send_sem=dsend.at[h * NS + a],
            recv_sem=drecv.at[h * NS + a],
            device_id={"pair": mirror, "blk": other},
            device_id_type=MESH,
        )

    for phase in range(2):
        h = half if phase == 0 else 1 - half

        def take(k, _):
            source = h * hp + (place - k + hp) % hp
            arrived(source).wait_recv()
            forward(source).start()
            return 0

        lax.fori_loop(1 - phase, hp, take, 0)

        def pass_on(k, _):
            handed(h * hp + k).wait_recv()
            return 0

        lax.fori_loop(0, hp, pass_on, 0)

        def build(k, _):
            group = h * hg + k
            entries = ebuf[pl.ds(pl.multiple_of(group * depth, SUB), depth), :]
            blocks = dot(fold_ref[...], entries).astype(jnp.bfloat16)
            rows = pl.ds(pl.multiple_of(group * SUB, SUB), SUB)
            for c in range(2):
                for a in range(NS):
                    for b in range(NS):
                        first = ((c * NS + a) * NS + b) * SUB
                        obuf[c, a, rows, b * NV : (b + 1) * NV] = blocks[first : first + SUB]
            return 0

        lax.fori_loop(0, hg, build, 0)
        if phase == 0:
            prop_copy.wait()
        rows = pl.ds(pl.multiple_of(h * hrows, hrows), hrows)

        def dress(j, _):
            x = (j + half) % 2
            columns = pl.ds(pl.multiple_of(x * NV, NV), NV)
            oreal = obuf[0, :, rows, :].reshape(NS * hrows, NS * NV)
            oimag = obuf[1, :, rows, :].reshape(NS * hrows, NS * NV)
            preal = pbuf[0, :, columns]
            pimag = pbuf[1, :, columns]
            dreal = dot(oreal, preal) - dot(oimag, pimag)
            dbuf[0, :, x, rows, :] = dreal.astype(jnp.bfloat16).reshape(NS, hrows, NV)
            dimag = dot(oreal, pimag) + dot(oimag, preal)
            dbuf[1, :, x, rows, :] = dimag.astype(jnp.bfloat16).reshape(NS, hrows, NV)
            block_copy(h, j).start()
            block_copy(h, j + 2).start()
            return 0

        lax.fori_loop(0, 2, dress, 0)

    row = lax.broadcasted_iota(jnp.int32, (hrows, NV), 0)
    column = lax.broadcasted_iota(jnp.int32, (hrows, NV), 1)
    total_real = jnp.zeros((hrows, NV), jnp.float32)
    total_imag = jnp.zeros((hrows, NV), jnp.float32)
    for phase in range(2):
        h = 1 - half if phase == 0 else half
        rows = pl.ds(pl.multiple_of(h * hrows, hrows), hrows)

        def close(a, carry):
            sum_real, sum_imag = carry
            block_arrived(h, a).wait_recv()
            x = (a + half + 1) % 2
            rreal, rimag = rbuf[0, a, rows, :], rbuf[1, a, rows, :]
            dreal, dimag = dbuf[0, a, x], dbuf[1, a, x]
            sum_real += dot(rreal, dreal) - dot(rimag, dimag)
            sum_imag += dot(rreal, dimag) + dot(rimag, dreal)
            return sum_real, sum_imag

        zero = jnp.zeros((hrows, NV), jnp.float32)
        sum_real, sum_imag = lax.fori_loop(0, NS, close, (zero, zero))
        diagonal = row + h * hrows == column
        total_real += jnp.where(diagonal, sum_real, 0.0)
        total_imag += jnp.where(diagonal, sum_imag, 0.0)
    real = jnp.sum(total_real)
    imag = jnp.sum(total_imag)
    lane = lax.broadcasted_iota(jnp.int32, (8, 128), 1)
    mine = half * 2 + core
    tot[mine] = jnp.where(lane == 0, real, jnp.where(lane == 1, imag, 0.0))

    def share(n, pair, blk):
        return pltpu.make_async_remote_copy(
            src_ref=tot.at[mine],
            dst_ref=tot.at[mine],
            send_sem=ssend.at[n],
            recv_sem=srecv.at[mine],
            device_id={"pair": pair, "blk": blk},
            device_id_type=MESH,
        )

    def shared(source):
        return pltpu.make_async_remote_copy(
            src_ref=tot.at[source],
            dst_ref=tot.at[source],
            send_sem=ssend.at[0],
            recv_sem=srecv.at[source],
            device_id={"pair": me, "blk": other},
            device_id_type=MESH,
        )

    shares = [share(0, me, other), share(1, mirror, core), share(2, mirror, other)]
    for copy in shares:
        copy.start()

    def sent(k, _):
        send_copy((me + k) % peers).wait_send()
        return 0

    lax.fori_loop(1, peers, sent, 0)

    def forwarded(k, _):
        forward(k).wait_send()
        return 0

    lax.fori_loop(0, peers, forwarded, 0)
    for h in range(2):
        for a in range(NS):
            block_copy(h, a).wait_send()
    for copy in shares:
        copy.wait_send()
    for source in (half * 2 + other, (1 - half) * 2 + core, (1 - half) * 2 + other):
        shared(source).wait_recv()
    out_ref[...] = ((tot[0] + tot[1]) + (tot[2] + tot[3]))[0:1, 0:2]


def shards(elementals, perambulator, pairs, elem_index, coef_code, term_count):
    peers = lax.axis_size("pair")
    me = lax.axis_index("pair")
    _, nops, parts, entries = elementals.shape
    lines = entries // NV
    sources = SUB // lines
    nterms = elem_index.shape[1]
    columns = perambulator.shape[-1]
    picked = elementals[pairs[:, 0]].reshape(peers, nops * parts * lines, NV)
    used = (jnp.arange(nterms) < term_count[me]).astype(jnp.float32)
    hot = (elem_index[me][:, None] == jnp.arange(nops)[None, :]).astype(jnp.float32)
    weights = coef_code[me].astype(jnp.float32) * 0.5 * used[:, None, None]
    merged = jnp.sum(hot[:, :, None, None] * weights[:, None], axis=0)
    same_part = jnp.eye(parts, dtype=jnp.float32)
    same_line = jnp.eye(SUB, dtype=jnp.float32).reshape(sources, lines, sources, lines)
    fold = (
        merged.transpose(1, 2, 0)[None, :, :, None, None, None, :, None, None]
        * same_part[:, None, None, None, None, None, None, :, None]
        * same_line[None, None, None, :, :, :, None, None, :]
    )
    depth = sources * nops * parts * lines
    fold = fold.astype(jnp.bfloat16).reshape(parts * NS * NS * SUB, depth)
    half_lines = NV
    return pl.pallas_call(
        functools.partial(kernel, peers),
        out_shape=jax.ShapeDtypeStruct((1, 2), jnp.float32),
        in_specs=[
            pl.BlockSpec(memory_space=pl.ANY),
            pl.BlockSpec(memory_space=pltpu.VMEM),
            pl.BlockSpec(memory_space=pl.ANY),
        ],
        out_specs=pl.BlockSpec(memory_space=pltpu.VMEM),
        scratch_shapes=[
            pltpu.VMEM((peers * 2 * nops * parts * lines, NV), jnp.bfloat16),
            pltpu.VMEM((2, NS, NV, NS * NV), jnp.bfloat16),
            pltpu.VMEM((2, NS * NV, columns), jnp.bfloat16),
            pltpu.VMEM((2, NS, 2, NV, NV), jnp.bfloat16),
            pltpu.VMEM((2, NS, half_lines, NV), jnp.bfloat16),
            pltpu.VMEM((4, 8, 128), jnp.float32),
            pltpu.SemaphoreType.DMA,
            pltpu.SemaphoreType.DMA,
            pltpu.SemaphoreType.DMA((peers,)),
            pltpu.SemaphoreType.DMA((peers,)),
            pltpu.SemaphoreType.DMA((peers,)),
            pltpu.SemaphoreType.DMA((peers,)),
            pltpu.SemaphoreType.DMA((2 * NS,)),
            pltpu.SemaphoreType.DMA((2 * NS,)),
            pltpu.SemaphoreType.DMA((3,)),
            pltpu.SemaphoreType.DMA((4,)),
        ],
        compiler_params=pltpu.CompilerParams(
            collective_id=0, has_side_effects=True, vmem_limit_bytes=48 * 1024 * 1024
        ),
    )(picked, fold, perambulator[0])


def solution(mesh):
    return jax.shard_map(
        shards,
        mesh=mesh,
        in_specs=(
            P("cfg", None, None, ("pair", "blk")),
            P(("cfg", "pair"), None, None, "blk"),
            P(),
            P(),
            P(),
            P(),
        ),
        out_specs=P(("cfg", "pair"), None),
        check_vma=False,
    )
```

```python
import functools

import jax
import jax.numpy as jnp
from jax import lax
from jax.experimental import pallas as pl
from jax.experimental.pallas import tpu as pltpu
from jax.sharding import PartitionSpec as P

NV = 256
NS = 4
SUB = 16
MESH = pl.DeviceIdType.MESH


def dot(x, y):
    return jnp.dot(x, y, preferred_element_type=jnp.float32)


def kernel(
    peers,
    lines,
    pairs_ref,
    count_ref,
    index_ref,
    code_ref,
    elem_ref,
    prop_ref,
    out_ref,
    sbuf,
    fold_ref,
    ebuf,
    obuf,
    pbuf,
    dbuf,
    rbuf,
    tot,
    psem,
    esend,
    erecv,
    fsend,
    frecv,
    dsend,
    drecv,
    ssend,
    srecv,
):
    me = lax.axis_index("pair")
    core = lax.axis_index("blk")
    other = 1 - core
    hp = peers // 2
    half = me // hp
    place = me % hp
    mirror = (me + hp) % peers
    chunk = elem_ref.shape[1]
    depth = fold_ref.shape[1]
    groups = peers * 2 * chunk // depth
    hg = groups // 2
    hrows = NV // 2

    prop_copy = pltpu.make_async_copy(prop_ref, pbuf, psem)
    prop_copy.start()

    def slot(s, c):
        return ebuf.at[pl.ds(pl.multiple_of((s * 2 + c) * chunk, SUB), chunk)]

    barrier = pltpu.get_barrier_semaphore()

    def greet(k, _):
        pl.semaphore_signal(
            barrier,
            inc=1,
            device_id={"pair": (me + k) % peers, "blk": core},
            device_id_type=MESH,
        )
        return 0

    lax.fori_loop(1, peers, greet, 0)
    for target in (me, mirror):
        pl.semaphore_signal(
            barrier, inc=1, device_id={"pair": target, "blk": other}, device_id_type=MESH
        )
    pl.semaphore_wait(barrier, peers + 1)

    def send_copy(target):
        return pltpu.make_async_remote_copy(
            src_ref=sbuf.at[target],
            dst_ref=slot(me, core),
            send_sem=esend.at[target],
            recv_sem=erecv.at[me],
            device_id={"pair": target, "blk": core},
            device_id_type=MESH,
        )

    def arrived(source):
        return pltpu.make_async_remote_copy(
            src_ref=slot(source, core),
            dst_ref=slot(source, core),
            send_sem=esend.at[source],
            recv_sem=erecv.at[source],
            device_id={"pair": me, "blk": other},
            device_id_type=MESH,
        )

    def forward(source):
        return pltpu.make_async_remote_copy(
            src_ref=slot(source, core),
            dst_ref=slot(source, core),
            send_sem=fsend.at[source],
            recv_sem=frecv.at[source],
            device_id={"pair": me, "blk": other},
            device_id_type=MESH,
        )

    def handed(source):
        return pltpu.make_async_remote_copy(
            src_ref=slot(source, other),
            dst_ref=slot(source, other),
            send_sem=fsend.at[source],
            recv_sem=frecv.at[source],
            device_id={"pair": me, "blk": other},
            device_id_type=MESH,
        )

    def post(target):
        sbuf[target] = elem_ref[pairs_ref[target, 0]]
        send_copy(target).start()

    post((1 - half) * hp + place)
    own_rows = pl.ds(pl.multiple_of((me * 2 + core) * chunk, SUB), chunk)
    ebuf[own_rows, :] = elem_ref[pairs_ref[me, 0]]
    forward(me).start()

    def send(k, _):
        step = (place + k) % hp
        post((1 - half) * hp + step)
        post(half * hp + step)
        return 0

    lax.fori_loop(1, hp, send, 0)

    nterms = index_ref.shape[1]
    rows = fold_ref.shape[0]
    spin = lax.broadcasted_iota(jnp.int32, (rows, NS * NS), 0) // SUB % (NS * NS)
    pick = (spin == lax.broadcasted_iota(jnp.int32, (rows, NS * NS), 1)).astype(jnp.float32)
    codes = code_ref[me].astype(jnp.float32).astype(jnp.bfloat16)
    spread = lax.dot_general(
        pick.astype(jnp.bfloat16),
        codes,
        (((1,), (1,)), ((), ())),
        preferred_element_type=jnp.float32,
    ).astype(jnp.bfloat16)
    entry = lax.broadcasted_iota(jnp.int32, (depth, nterms), 0) % chunk // (2 * lines)
    term = lax.broadcasted_iota(jnp.int32, (depth, nterms), 1)
    uses = (entry == index_ref[pl.ds(me, 1), :]) & (term < count_ref[me])
    halves = jnp.where(uses, 0.5, 0.0).astype(jnp.bfloat16)
    weights = lax.dot_general(
        spread, halves, (((1,), (1,)), ((), ())), preferred_element_type=jnp.float32
    )
    out_row = lax.broadcasted_iota(jnp.int32, (rows, depth), 0)
    in_row = lax.broadcasted_iota(jnp.int32, (rows, depth), 1)
    same_part = out_row // (NS * NS * SUB) == in_row // lines % 2
    same_line = out_row % SUB == in_row // chunk * lines + in_row % lines
    fold_ref[...] = jnp.where(same_part & same_line, weights, 0.0).astype(jnp.bfloat16)

    def block_copy(h, a):
        x = (a + half) % 2
        place_there = 2 * core + x
        return pltpu.make_async_remote_copy(
            src_ref=dbuf.at[:, a, x, pl.ds(pl.multiple_of(h * hrows, hrows), hrows)],
            dst_ref=rbuf.at[:, place_there, pl.ds(pl.multiple_of(h * hrows, hrows), hrows)],
            send_sem=dsend.at[h * NS + a],
            recv_sem=drecv.at[h * NS + place_there],
            device_id={"pair": mirror, "blk": a // 2},
            device_id_type=MESH,
        )

    def block_arrived(h, a):
        rows = pl.ds(pl.multiple_of(h * hrows, hrows), hrows)
        return pltpu.make_async_remote_copy(
            src_ref=rbuf.at[:, a, rows],
            dst_ref=rbuf.at[:, a, rows],
            send_sem=dsend.at[h * NS + a],
            recv_sem=drecv.at[h * NS + a],
            device_id={"pair": mirror, "blk": other},
            device_id_type=MESH,
        )

    for phase in range(2):
        h = half if phase == 0 else 1 - half

        def take(k, _):
            source = h * hp + (place - k + hp) % hp
            arrived(source).wait_recv()
            forward(source).start()
            return 0

        lax.fori_loop(1 - phase, hp, take, 0)

        def pass_on(k, _):
            handed(h * hp + k).wait_recv()
            return 0

        lax.fori_loop(0, hp, pass_on, 0)

        def build(k, _):
            group = h * hg + k
            entries = ebuf[pl.ds(pl.multiple_of(group * depth, SUB), depth), :]
            blocks = dot(fold_ref[...], entries).astype(jnp.bfloat16)
            rows = pl.ds(pl.multiple_of(group * SUB, SUB), SUB)
            for c in range(2):
                for a in range(NS):
                    for b in range(NS):
                        first = ((c * NS + a) * NS + b) * SUB
                        obuf[c, a, rows, b * NV : (b + 1) * NV] = blocks[first : first + SUB]
            return 0

        lax.fori_loop(0, hg, build, 0)
        if phase == 0:
            prop_copy.wait()
        rows = pl.ds(pl.multiple_of(h * hrows, hrows), hrows)

        def dress(j, _):
            x = (j + half) % 2
            columns = pl.ds(pl.multiple_of(x * NV, NV), NV)
            oreal = obuf[0, :, rows, :].reshape(NS * hrows, NS * NV)
            oimag = obuf[1, :, rows, :].reshape(NS * hrows, NS * NV)
            preal = pbuf[0, :, columns]
            pimag = pbuf[1, :, columns]
            dreal = dot(oreal, preal) - dot(oimag, pimag)
            dbuf[0, :, x, rows, :] = dreal.astype(jnp.bfloat16).reshape(NS, hrows, NV)
            dimag = dot(oreal, pimag) + dot(oimag, preal)
            dbuf[1, :, x, rows, :] = dimag.astype(jnp.bfloat16).reshape(NS, hrows, NV)
            block_copy(h, j).start()
            block_copy(h, j + 2).start()
            return 0

        lax.fori_loop(0, 2, dress, 0)

    row = lax.broadcasted_iota(jnp.int32, (hrows, NV), 0)
    column = lax.broadcasted_iota(jnp.int32, (hrows, NV), 1)
    total_real = jnp.zeros((hrows, NV), jnp.float32)
    total_imag = jnp.zeros((hrows, NV), jnp.float32)
    for phase in range(2):
        h = 1 - half if phase == 0 else half
        rows = pl.ds(pl.multiple_of(h * hrows, hrows), hrows)

        def close(a, carry):
            sum_real, sum_imag = carry
            block_arrived(h, a).wait_recv()
            x = (a + half + 1) % 2
            rreal, rimag = rbuf[0, a, rows, :], rbuf[1, a, rows, :]
            dreal, dimag = dbuf[0, a, x], dbuf[1, a, x]
            sum_real += dot(rreal, dreal) - dot(rimag, dimag)
            sum_imag += dot(rreal, dimag) + dot(rimag, dreal)
            return sum_real, sum_imag

        zero = jnp.zeros((hrows, NV), jnp.float32)
        sum_real, sum_imag = lax.fori_loop(0, NS, close, (zero, zero))
        diagonal = row + h * hrows == column
        total_real += jnp.where(diagonal, sum_real, 0.0)
        total_imag += jnp.where(diagonal, sum_imag, 0.0)
    real = jnp.sum(total_real)
    imag = jnp.sum(total_imag)
    lane = lax.broadcasted_iota(jnp.int32, (8, 128), 1)
    mine = half * 2 + core
    tot[mine] = jnp.where(lane == 0, real, jnp.where(lane == 1, imag, 0.0))

    def share(n, pair, blk):
        return pltpu.make_async_remote_copy(
            src_ref=tot.at[mine],
            dst_ref=tot.at[mine],
            send_sem=ssend.at[n],
            recv_sem=srecv.at[mine],
            device_id={"pair": pair, "blk": blk},
            device_id_type=MESH,
        )

    def shared(source):
        return pltpu.make_async_remote_copy(
            src_ref=tot.at[source],
            dst_ref=tot.at[source],
            send_sem=ssend.at[0],
            recv_sem=srecv.at[source],
            device_id={"pair": me, "blk": other},
            device_id_type=MESH,
        )

    shares = [share(0, me, other), share(1, mirror, core), share(2, mirror, other)]
    for copy in shares:
        copy.start()

    def sent(k, _):
        send_copy((me + k) % peers).wait_send()
        return 0

    lax.fori_loop(1, peers, sent, 0)

    def forwarded(k, _):
        forward(k).wait_send()
        return 0

    lax.fori_loop(0, peers, forwarded, 0)
    for h in range(2):
        for a in range(NS):
            block_copy(h, a).wait_send()
    for copy in shares:
        copy.wait_send()
    for source in (half * 2 + other, (1 - half) * 2 + core, (1 - half) * 2 + other):
        shared(source).wait_recv()
    out_ref[...] = ((tot[0] + tot[1]) + (tot[2] + tot[3]))[0:1, 0:2]


def shards(elementals, perambulator, pairs, elem_index, coef_code, term_count):
    peers = lax.axis_size("pair")
    _, nops, parts, entries = elementals.shape
    lines = entries // NV
    sources = SUB // lines
    nterms = elem_index.shape[1]
    columns = perambulator.shape[-1]
    chunk = nops * parts * lines
    slices = elementals.reshape(elementals.shape[0], chunk, NV)
    codes = coef_code.reshape(peers, nterms, NS * NS)
    return pl.pallas_call(
        functools.partial(kernel, peers, lines),
        out_shape=jax.ShapeDtypeStruct((1, 2), jnp.float32),
        in_specs=[
            pl.BlockSpec(memory_space=pltpu.SMEM),
            pl.BlockSpec(memory_space=pltpu.SMEM),
            pl.BlockSpec(memory_space=pltpu.VMEM),
            pl.BlockSpec(memory_space=pltpu.VMEM),
            pl.BlockSpec(memory_space=pltpu.VMEM),
            pl.BlockSpec(memory_space=pl.ANY),
        ],
        out_specs=pl.BlockSpec(memory_space=pltpu.VMEM),
        scratch_shapes=[
            pltpu.VMEM((peers, chunk, NV), jnp.bfloat16),
            pltpu.VMEM((parts * NS * NS * SUB, sources * chunk), jnp.bfloat16),
            pltpu.VMEM((peers * 2 * chunk, NV), jnp.bfloat16),
            pltpu.VMEM((2, NS, NV, NS * NV), jnp.bfloat16),
            pltpu.VMEM((2, NS * NV, columns), jnp.bfloat16),
            pltpu.VMEM((2, NS, 2, NV, NV), jnp.bfloat16),
            pltpu.VMEM((2, NS, NV, NV), jnp.bfloat16),
            pltpu.VMEM((4, 8, 128), jnp.float32),
            pltpu.SemaphoreType.DMA,
            pltpu.SemaphoreType.DMA((peers,)),
            pltpu.SemaphoreType.DMA((peers,)),
            pltpu.SemaphoreType.DMA((peers,)),
            pltpu.SemaphoreType.DMA((peers,)),
            pltpu.SemaphoreType.DMA((2 * NS,)),
            pltpu.SemaphoreType.DMA((2 * NS,)),
            pltpu.SemaphoreType.DMA((3,)),
            pltpu.SemaphoreType.DMA((4,)),
        ],
        compiler_params=pltpu.CompilerParams(
            collective_id=0, has_side_effects=True, vmem_limit_bytes=48 * 1024 * 1024
        ),
    )(pairs, term_count, elem_index, codes, slices, perambulator[0])


def solution(mesh):
    return jax.shard_map(
        shards,
        mesh=mesh,
        in_specs=(
            P("cfg", None, None, ("pair", "blk")),
            P(("cfg", "pair"), None, None, "blk"),
            P(),
            P(),
            P(),
            P(),
        ),
        out_specs=P(("cfg", "pair"), None),
        check_vma=False,
    )
```

```python
import functools

import jax
import jax.numpy as jnp
from jax import lax
from jax.experimental import pallas as pl
from jax.experimental.pallas import tpu as pltpu
from jax.sharding import PartitionSpec as P

NV = 256
NS = 4
SUB = 16
MESH = pl.DeviceIdType.MESH


def dot(x, y):
    return jnp.dot(x, y, preferred_element_type=jnp.float32)


def kernel(
    peers,
    lines,
    pairs_ref,
    count_ref,
    index_ref,
    code_ref,
    elem_ref,
    prop_ref,
    out_ref,
    sbuf,
    fold_ref,
    ebuf,
    obuf,
    pbuf,
    dbuf,
    rbuf,
    tot,
    psem,
    esend,
    erecv,
    fsend,
    frecv,
    dsend,
    drecv,
    ssend,
    srecv,
):
    me = lax.axis_index("pair")
    core = lax.axis_index("blk")
    other = 1 - core
    hp = peers // 2
    half = me // hp
    place = me % hp
    mirror = (me + hp) % peers
    chunk = elem_ref.shape[1]
    depth = fold_ref.shape[1]
    groups = peers * 2 * chunk // depth
    hg = groups // 2
    hrows = NV // 2

    prop_copy = pltpu.make_async_copy(prop_ref, pbuf, psem)
    prop_copy.start()

    def slot(s, c):
        return ebuf.at[pl.ds(pl.multiple_of((s * 2 + c) * chunk, SUB), chunk)]

    barrier = pltpu.get_barrier_semaphore()

    def greet(k, _):
        pl.semaphore_signal(
            barrier,
            inc=1,
            device_id={"pair": (me + k) % peers, "blk": core},
            device_id_type=MESH,
        )
        return 0

    lax.fori_loop(1, peers, greet, 0)
    for target in (me, mirror):
        pl.semaphore_signal(
            barrier, inc=1, device_id={"pair": target, "blk": other}, device_id_type=MESH
        )

    def fill(k, _):
        sbuf[k] = elem_ref[pairs_ref[k, 0]]
        return 0

    lax.fori_loop(0, peers, fill, 0)
    own_rows = pl.ds(pl.multiple_of((me * 2 + core) * chunk, SUB), chunk)
    ebuf[own_rows, :] = elem_ref[pairs_ref[me, 0]]
    pl.semaphore_wait(barrier, peers + 1)

    def send_copy(target):
        return pltpu.make_async_remote_copy(
            src_ref=sbuf.at[target],
            dst_ref=slot(me, core),
            send_sem=esend.at[target],
            recv_sem=erecv.at[me],
            device_id={"pair": target, "blk": core},
            device_id_type=MESH,
        )

    def arrived(source):
        return pltpu.make_async_remote_copy(
            src_ref=slot(source, core),
            dst_ref=slot(source, core),
            send_sem=esend.at[source],
            recv_sem=erecv.at[source],
            device_id={"pair": me, "blk": other},
            device_id_type=MESH,
        )

    def forward(source):
        return pltpu.make_async_remote_copy(
            src_ref=slot(source, core),
            dst_ref=slot(source, core),
            send_sem=fsend.at[source],
            recv_sem=frecv.at[source],
            device_id={"pair": me, "blk": other},
            device_id_type=MESH,
        )

    def handed(source):
        return pltpu.make_async_remote_copy(
            src_ref=slot(source, other),
            dst_ref=slot(source, other),
            send_sem=fsend.at[source],
            recv_sem=frecv.at[source],
            device_id={"pair": me, "blk": other},
            device_id_type=MESH,
        )

    def near(k):
        send_copy(half * hp + (place + k) % hp).start()

    def far(k):
        send_copy((1 - half) * hp + (place + k) % hp).start()

    def send_mixed(k, _):
        far(k)
        near(2 * k + 1)
        near(2 * k + 2)
        return 0

    def send_far(k, _):
        far(k)
        return 0

    mixed = (hp - 1) // 2
    lax.fori_loop(0, mixed, send_mixed, 0)
    forward(me).start()
    far(mixed)
    near(hp - 1)
    lax.fori_loop(mixed + 1, hp, send_far, 0)

    nterms = index_ref.shape[1]
    rows = fold_ref.shape[0]
    spin = lax.broadcasted_iota(jnp.int32, (rows, NS * NS), 0) // SUB % (NS * NS)
    pick = (spin == lax.broadcasted_iota(jnp.int32, (rows, NS * NS), 1)).astype(jnp.float32)
    codes = code_ref[me].astype(jnp.float32).astype(jnp.bfloat16)
    spread = lax.dot_general(
        pick.astype(jnp.bfloat16),
        codes,
        (((1,), (1,)), ((), ())),
        preferred_element_type=jnp.float32,
    ).astype(jnp.bfloat16)
    entry = lax.broadcasted_iota(jnp.int32, (depth, nterms), 0) % chunk // (2 * lines)
    term = lax.broadcasted_iota(jnp.int32, (depth, nterms), 1)
    uses = (entry == index_ref[pl.ds(me, 1), :]) & (term < count_ref[me])
    halves = jnp.where(uses, 0.5, 0.0).astype(jnp.bfloat16)
    weights = lax.dot_general(
        spread, halves, (((1,), (1,)), ((), ())), preferred_element_type=jnp.float32
    )
    out_row = lax.broadcasted_iota(jnp.int32, (rows, depth), 0)
    in_row = lax.broadcasted_iota(jnp.int32, (rows, depth), 1)
    same_part = out_row // (NS * NS * SUB) == in_row // lines % 2
    same_line = out_row % SUB == in_row // chunk * lines + in_row % lines
    fold_ref[...] = jnp.where(same_part & same_line, weights, 0.0).astype(jnp.bfloat16)

    def block_copy(h, a):
        x = (a + half) % 2
        place_there = 2 * core + x
        return pltpu.make_async_remote_copy(
            src_ref=dbuf.at[:, a, x, pl.ds(pl.multiple_of(h * hrows, hrows), hrows)],
            dst_ref=rbuf.at[:, place_there, pl.ds(pl.multiple_of(h * hrows, hrows), hrows)],
            send_sem=dsend.at[h * NS + a],
            recv_sem=drecv.at[h * NS + place_there],
            device_id={"pair": mirror, "blk": a // 2},
            device_id_type=MESH,
        )

    def block_arrived(h, a):
        rows = pl.ds(pl.multiple_of(h * hrows, hrows), hrows)
        return pltpu.make_async_remote_copy(
            src_ref=rbuf.at[:, a, rows],
            dst_ref=rbuf.at[:, a, rows],
            send_sem=dsend.at[h * NS + a],
            recv_sem=drecv.at[h * NS + a],
            device_id={"pair": mirror, "blk": other},
            device_id_type=MESH,
        )

    for phase in range(2):
        h = half if phase == 0 else 1 - half

        def take(k, _):
            source = h * hp + (place - k + hp) % hp
            arrived(source).wait_recv()
            forward(source).start()
            return 0

        lax.fori_loop(1 - phase, hp, take, 0)

        def pass_on(k, _):
            handed(h * hp + k).wait_recv()
            return 0

        lax.fori_loop(0, hp, pass_on, 0)

        def build(k, _):
            group = h * hg + k
            entries = ebuf[pl.ds(pl.multiple_of(group * depth, SUB), depth), :]
            blocks = dot(fold_ref[...], entries).astype(jnp.bfloat16)
            rows = pl.ds(pl.multiple_of(group * SUB, SUB), SUB)
            for c in range(2):
                for a in range(NS):
                    for b in range(NS):
                        first = ((c * NS + a) * NS + b) * SUB
                        obuf[c, a, rows, b * NV : (b + 1) * NV] = blocks[first : first + SUB]
            return 0

        lax.fori_loop(0, hg, build, 0)
        if phase == 0:
            prop_copy.wait()
        rows = pl.ds(pl.multiple_of(h * hrows, hrows), hrows)

        def dress(j, _):
            x = (j + half) % 2
            columns = pl.ds(pl.multiple_of(x * NV, NV), NV)
            oreal = obuf[0, :, rows, :].reshape(NS * hrows, NS * NV)
            oimag = obuf[1, :, rows, :].reshape(NS * hrows, NS * NV)
            preal = pbuf[0, :, columns]
            pimag = pbuf[1, :, columns]
            dreal = dot(oreal, preal) - dot(oimag, pimag)
            dbuf[0, :, x, rows, :] = dreal.astype(jnp.bfloat16).reshape(NS, hrows, NV)
            dimag = dot(oreal, pimag) + dot(oimag, preal)
            dbuf[1, :, x, rows, :] = dimag.astype(jnp.bfloat16).reshape(NS, hrows, NV)
            block_copy(h, j).start()
            block_copy(h, j + 2).start()
            return 0

        lax.fori_loop(0, 2, dress, 0)

    row = lax.broadcasted_iota(jnp.int32, (hrows, NV), 0)
    column = lax.broadcasted_iota(jnp.int32, (hrows, NV), 1)
    total_real = jnp.zeros((hrows, NV), jnp.float32)
    total_imag = jnp.zeros((hrows, NV), jnp.float32)
    for phase in range(2):
        h = 1 - half if phase == 0 else half
        rows = pl.ds(pl.multiple_of(h * hrows, hrows), hrows)

        def close(a, carry):
            sum_real, sum_imag = carry
            block_arrived(h, a).wait_recv()
            x = (a + half + 1) % 2
            rreal, rimag = rbuf[0, a, rows, :], rbuf[1, a, rows, :]
            dreal, dimag = dbuf[0, a, x], dbuf[1, a, x]
            sum_real += dot(rreal, dreal) - dot(rimag, dimag)
            sum_imag += dot(rreal, dimag) + dot(rimag, dreal)
            return sum_real, sum_imag

        zero = jnp.zeros((hrows, NV), jnp.float32)
        sum_real, sum_imag = lax.fori_loop(0, NS, close, (zero, zero))
        diagonal = row + h * hrows == column
        total_real += jnp.where(diagonal, sum_real, 0.0)
        total_imag += jnp.where(diagonal, sum_imag, 0.0)
    real = jnp.sum(total_real)
    imag = jnp.sum(total_imag)
    lane = lax.broadcasted_iota(jnp.int32, (8, 128), 1)
    mine = half * 2 + core
    tot[mine] = jnp.where(lane == 0, real, jnp.where(lane == 1, imag, 0.0))

    def share(n, pair, blk):
        return pltpu.make_async_remote_copy(
            src_ref=tot.at[mine],
            dst_ref=tot.at[mine],
            send_sem=ssend.at[n],
            recv_sem=srecv.at[mine],
            device_id={"pair": pair, "blk": blk},
            device_id_type=MESH,
        )

    def shared(source):
        return pltpu.make_async_remote_copy(
            src_ref=tot.at[source],
            dst_ref=tot.at[source],
            send_sem=ssend.at[0],
            recv_sem=srecv.at[source],
            device_id={"pair": me, "blk": other},
            device_id_type=MESH,
        )

    shares = [share(0, me, other), share(1, mirror, core), share(2, mirror, other)]
    for copy in shares:
        copy.start()

    def sent(k, _):
        send_copy((me + k) % peers).wait_send()
        return 0

    lax.fori_loop(1, peers, sent, 0)

    def forwarded(k, _):
        forward(k).wait_send()
        return 0

    lax.fori_loop(0, peers, forwarded, 0)
    for h in range(2):
        for a in range(NS):
            block_copy(h, a).wait_send()
    for copy in shares:
        copy.wait_send()
    for source in (half * 2 + other, (1 - half) * 2 + core, (1 - half) * 2 + other):
        shared(source).wait_recv()
    out_ref[...] = ((tot[0] + tot[1]) + (tot[2] + tot[3]))[0:1, 0:2]


def shards(elementals, perambulator, pairs, elem_index, coef_code, term_count):
    peers = lax.axis_size("pair")
    _, nops, parts, entries = elementals.shape
    lines = entries // NV
    sources = SUB // lines
    nterms = elem_index.shape[1]
    columns = perambulator.shape[-1]
    chunk = nops * parts * lines
    slices = elementals.reshape(elementals.shape[0], chunk, NV)
    codes = coef_code.reshape(peers, nterms, NS * NS)
    return pl.pallas_call(
        functools.partial(kernel, peers, lines),
        out_shape=jax.ShapeDtypeStruct((1, 2), jnp.float32),
        in_specs=[
            pl.BlockSpec(memory_space=pltpu.SMEM),
            pl.BlockSpec(memory_space=pltpu.SMEM),
            pl.BlockSpec(memory_space=pltpu.VMEM),
            pl.BlockSpec(memory_space=pltpu.VMEM),
            pl.BlockSpec(memory_space=pltpu.VMEM),
            pl.BlockSpec(memory_space=pl.ANY),
        ],
        out_specs=pl.BlockSpec(memory_space=pltpu.VMEM),
        scratch_shapes=[
            pltpu.VMEM((peers, chunk, NV), jnp.bfloat16),
            pltpu.VMEM((parts * NS * NS * SUB, sources * chunk), jnp.bfloat16),
            pltpu.VMEM((peers * 2 * chunk, NV), jnp.bfloat16),
            pltpu.VMEM((2, NS, NV, NS * NV), jnp.bfloat16),
            pltpu.VMEM((2, NS * NV, columns), jnp.bfloat16),
            pltpu.VMEM((2, NS, 2, NV, NV), jnp.bfloat16),
            pltpu.VMEM((2, NS, NV, NV), jnp.bfloat16),
            pltpu.VMEM((4, 8, 128), jnp.float32),
            pltpu.SemaphoreType.DMA,
            pltpu.SemaphoreType.DMA((peers,)),
            pltpu.SemaphoreType.DMA((peers,)),
            pltpu.SemaphoreType.DMA((peers,)),
            pltpu.SemaphoreType.DMA((peers,)),
            pltpu.SemaphoreType.DMA((2 * NS,)),
            pltpu.SemaphoreType.DMA((2 * NS,)),
            pltpu.SemaphoreType.DMA((3,)),
            pltpu.SemaphoreType.DMA((4,)),
        ],
        compiler_params=pltpu.CompilerParams(
            collective_id=0, has_side_effects=True, vmem_limit_bytes=48 * 1024 * 1024
        ),
    )(pairs, term_count, elem_index, codes, slices, perambulator[0])


def solution(mesh):
    return jax.shard_map(
        shards,
        mesh=mesh,
        in_specs=(
            P("cfg", None, None, ("pair", "blk")),
            P(("cfg", "pair"), None, None, "blk"),
            P(),
            P(),
            P(),
            P(),
        ),
        out_specs=P(("cfg", "pair"), None),
        check_vma=False,
    )
```
